256 devices in a mesh: dp: 64 (over z, x, core), tensor: 4 (over y).
Axes of the slice: x: 4, y: 4, z: 8, core: 2. Of those that a mesh axis runs over, the one named last changes fastest.
Arguments:
- layer_input: bfloat16 [49152, 3584], P(('dp', 'tensor')), may hold values from -1.5 to 1.5
- output_grad: bfloat16 [49152, 1024], P('dp', 'tensor'), may hold values from -6 to 6
- query_weight: bfloat16 [3584, 1024], P(None, 'tensor'), may hold values from -0.09375 to 0.09375
- error_buffer: bfloat16 [64, 3584, 1024], P('dp', None, 'tensor'), may hold values from -48 to 48
- right_prev: float32 [1024, 64], P('tensor'), may hold values from -6 to 6
Outputs:
- input_grad: bfloat16 [49152, 3584], P(('dp', 'tensor'))
- right_factor: float32 [1024, 64], P('tensor')
- error_next: bfloat16 [64, 3584, 1024], P('dp', None, 'tensor')
The draws below stay inside these ranges and needn't reach their ends.
All inputs are finite; a program needn't handle non-finite values.
Results may differ from the reference program's by a relative error of at most 0.0007.
Values may be sent and summed in bfloat16 or wider, within the bound.
No kernel may reach another device: no remote copies, remote signals or barrier semaphores. Data moves between devices by JAX's collectives and lax.ppermute only.
A program may use at most 128 MiB of HBM per device.

```python
import jax
import jax.numpy as jnp
from jax import lax

D = 3584
HEAD_DEV = 4
HEAD_SIZE = 64
RANK = 64
COLS = 1024
SEQ = 768
TOKENS = 49152
N_DP = 64
N_TENSOR = 4


def shard_levels(key, dims, shards, least, largest):
    factor_of, own = 1.0, jax.random.fold_in(key, 6)
    for axis_at, shards_of in shards:
        draws = jnp.exp(jax.random.uniform(jax.random.fold_in(own, axis_at), (shards_of,), jnp.float32, least / len(shards), largest / len(shards)))
        factor_of = factor_of * jnp.repeat(draws, dims[axis_at] // shards_of).reshape([-1 if axis == axis_at else 1 for axis in range(len(dims))])
    return factor_of


def bell_draw(rng, shape, deviation, reach, split=(), held_as=jnp.bfloat16):
    entries = jax.random.normal(rng, shape, jnp.float32) * deviation
    if len(split) > 0:
        entries = shard_levels(rng, shape, split, -0.22, 0.18) * entries
    return jnp.clip(entries, min=-reach, max=reach).astype(held_as)


def setup_inputs(seed: int = 0) -> dict:
    seeds = jax.random.split(jax.random.key(seed), 6)
    layer_input = bell_draw(seeds[0], (TOKENS, D), 0.25, 1.5, ((0, 256),))
    output_grad = bell_draw(seeds[1], (TOKENS, COLS), 1.0, 6.0, ((0, 64), (1, 4)))
    query_weight = bell_draw(seeds[2], (D, COLS), D ** -0.5, 0.09375, ((1, 4),))
    error_buffer = bell_draw(seeds[3], (N_DP, D, COLS), 8.0, 48.0, ((0, 64), (2, 4)))
    right_prev = bell_draw(seeds[4], (COLS, RANK), 1.0, 6.0, ((0, 4),), jnp.float32)
    return dict(layer_input=layer_input, output_grad=output_grad, query_weight=query_weight, error_buffer=error_buffer, right_prev=right_prev)


def build_merged(layer_input, output_grad, error_buffer, replica):
    token_rows = lax.dynamic_slice_in_dim(layer_input, replica * SEQ, SEQ, 0)
    grad_rows = lax.dynamic_slice_in_dim(output_grad, replica * SEQ, SEQ, 0)
    weight_grad = lax.dot_general(token_rows.astype(jnp.float32), grad_rows.astype(jnp.float32), (((0,), (0,)), ((), ())), preferred_element_type=jnp.float32)
    merged = weight_grad + error_buffer[replica].astype(jnp.float32)
    return merged.reshape(D, N_TENSOR, HEAD_DEV * HEAD_SIZE)

def orthonormal(left_block):
    gram_matrix = jnp.dot(left_block.T, left_block, precision=lax.Precision.HIGHEST)
    lower_factor = jnp.linalg.cholesky(gram_matrix)
    return jax.scipy.linalg.solve_triangular(lower_factor, left_block.T, lower=True).T

def reference(layer_input, output_grad, query_weight, error_buffer, right_prev):
    highest = lax.Precision.HIGHEST
    input_grad = lax.dot_general(output_grad.astype(jnp.float32), query_weight.astype(jnp.float32), (((1,), (1,)), ((), ())), preferred_element_type=jnp.float32).astype(jnp.bfloat16)
    right_blocks = right_prev.reshape(N_TENSOR, HEAD_DEV * HEAD_SIZE, RANK)
    replicas = jnp.arange(N_DP, dtype=jnp.int32)

    def left_step(running, replica):
        merged = build_merged(layer_input, output_grad, error_buffer, replica)
        return (running + jnp.einsum('dtc,tcr->tdr', merged, right_blocks, precision=highest), None)
    left_total, _ = lax.scan(left_step, jnp.zeros((N_TENSOR, D, RANK), jnp.float32), replicas)
    left_mean = left_total / N_DP
    left_basis = jax.vmap(orthonormal)(left_mean)

    def right_step(running, replica):
        merged = build_merged(layer_input, output_grad, error_buffer, replica)
        return (running + jnp.einsum('dtc,tdr->tcr', merged, left_basis, precision=highest), None)
    right_total, _ = lax.scan(right_step, jnp.zeros((N_TENSOR, HEAD_DEV * HEAD_SIZE, RANK), jnp.float32), replicas)
    right_blocks_new = right_total / N_DP
    approx = jnp.einsum('tdr,tcr->dtc', left_basis, right_blocks_new, precision=highest)

    def error_one(replica):
        merged = build_merged(layer_input, output_grad, error_buffer, replica)
        return (merged - approx).reshape(D, COLS).astype(jnp.bfloat16)
    error_next = lax.map(error_one, replicas)
    right_factor = right_blocks_new.reshape(COLS, RANK)
    return (input_grad, right_factor, error_next)
```

```python
import jax
import jax.numpy as jnp
from jax import lax
from jax.experimental import pallas as pl
from jax.experimental.pallas import tpu as pltpu
from jax.sharding import Mesh, PartitionSpec as P

F32, BF16 = jnp.float32, jnp.bfloat16
HIGHEST = lax.Precision.HIGHEST
FEATURES, COLUMNS, RANK, SEQ, PART = 3584, 256, 64, 768, 192
HALF = RANK // 2
REPLICAS = 64
PLANE = ("z", "x")
VMEM = pltpu.CompilerParams(vmem_limit_bytes=40 * 2**20)


def dot(a, b, dim_a, dim_b, precision=None):
    return lax.dot_general(
        a, b, (((dim_a,), (dim_b,)), ((), ())), precision=precision, preferred_element_type=F32
    )


def cost(flops, read):
    return pl.CostEstimate(flops=flops, bytes_accessed=read, transcendentals=0)


def whole(array):
    return pl.BlockSpec(array.shape, lambda i: (0,) * array.ndim)


def shift(value, axis, size, by):
    return lax.ppermute(value, axis, [(at, (at + by) % size) for at in range(size)])


def merged_and_left(pieces, grads, error, right, block):
    features = error.shape[0]

    def body(*refs):
        *piece_refs, grad_ref, error_ref, right_ref, merged_ref, left_ref = refs
        tokens = jnp.concatenate([ref[...] for ref in piece_refs], 0)
        transposed = dot(grad_ref[...], tokens, 0, 0)
        merged = transposed.T + error_ref[...].astype(F32)
        merged_ref[...] = merged
        left_ref[...] = dot(merged, right_ref[...], 1, 0, HIGHEST).T

    return pl.pallas_call(
        body,
        grid=(features // block,),
        in_specs=[pl.BlockSpec((piece.shape[0], block), lambda i: (0, i)) for piece in pieces]
        + [whole(grads), pl.BlockSpec((block, COLUMNS), lambda i: (i, 0)), whole(right)],
        out_specs=[
            pl.BlockSpec((block, COLUMNS), lambda i: (i, 0)),
            pl.BlockSpec((RANK, block), lambda i: (0, i)),
        ],
        out_shape=[
            jax.ShapeDtypeStruct((features, COLUMNS), F32),
            jax.ShapeDtypeStruct((RANK, features), F32),
        ],
        compiler_params=VMEM,
        cost_estimate=cost(4 * SEQ * features * COLUMNS, 8 * features * COLUMNS),
        name="merged_and_left",
    )(*pieces, grads, error, right)


def ordered(core, mine, other):
    first = core == 0
    return jnp.concatenate([jnp.where(first, mine, other), jnp.where(first, other, mine)], 0)


def products(core, mine, other, merged_parts, block):
    features = mine.shape[1]
    steps = features // block
    per_part = steps // len(merged_parts)

    def body(core_ref, mine_ref, other_ref, *refs):
        *merged_refs, left_ref, cross_ref, gram_ref = refs
        step = pl.program_id(0)

        @pl.when(step == 0)
        def _():
            cross_ref[...] = jnp.zeros_like(cross_ref)
            gram_ref[...] = jnp.zeros_like(gram_ref)

        left = ordered(core_ref[0], mine_ref[...], other_ref[...])
        left_ref[...] = left
        gram_ref[...] += dot(left, left, 1, 1, HIGHEST)
        for part, merged_ref in enumerate(merged_refs):

            @pl.when(step // per_part == part)
            def _():
                cross_ref[...] += dot(left, merged_ref[...], 1, 0, HIGHEST)

    def part_spec(part):
        return pl.BlockSpec(
            (block, COLUMNS), lambda i: (jnp.clip(i - part * per_part, 0, per_part - 1), 0)
        )

    rows = pl.BlockSpec((HALF, block), lambda i: (0, i))
    return pl.pallas_call(
        body,
        grid=(steps,),
        in_specs=[pl.BlockSpec(memory_space=pltpu.SMEM), rows, rows]
        + [part_spec(part) for part in range(len(merged_parts))],
        out_specs=[
            pl.BlockSpec((RANK, block), lambda i: (0, i)),
            pl.BlockSpec((RANK, COLUMNS), lambda i: (0, 0)),
            pl.BlockSpec((RANK, RANK), lambda i: (0, 0)),
        ],
        out_shape=[
            jax.ShapeDtypeStruct((RANK, features), F32),
            jax.ShapeDtypeStruct((RANK, COLUMNS), F32),
            jax.ShapeDtypeStruct((RANK, RANK), F32),
        ],
        compiler_params=VMEM,
        cost_estimate=cost(12 * features * COLUMNS * RANK, 5 * features * COLUMNS),
        name="cross_and_gram",
    )(core, mine, other, *merged_parts)


def inverse_factor(gram):
    def body(gram_ref, inverse_ref):
        rows = lax.broadcasted_iota(jnp.int32, (RANK, 2 * RANK), 0)
        lanes = lax.broadcasted_iota(jnp.int32, (RANK, 2 * RANK), 1)
        work = jnp.concatenate([gram_ref[...], jnp.zeros((RANK, RANK), F32)], 1)
        work = jnp.where(lanes == rows + RANK, 1.0, work)
        for at in range(RANK):
            pivot_row = work[at : at + 1, :]
            pivot = pivot_row[:, at : at + 1]
            inverse = 1.0 / jnp.sqrt(pivot)
            scaled = pivot_row * inverse
            factor = work[:, at : at + 1] * inverse
            work = jnp.where(
                rows > at, work - factor * scaled, jnp.where(rows == at, scaled, work)
            )
        inverse_ref[...] = work[:, RANK:]

    return pl.pallas_call(
        body,
        out_shape=jax.ShapeDtypeStruct((RANK, RANK), F32),
        cost_estimate=cost(10**7, 10**4),
        name="inverse_factor",
    )(gram)


def finish(core, mine, other, inverse, left, merged_parts, block):
    features = left.shape[1]
    steps = features // block
    per_part = steps // len(merged_parts)

    def body(core_ref, mine_ref, other_ref, inverse_ref, left_ref, *refs):
        *merged_refs, error_ref, right_ref, mix_ref = refs
        step = pl.program_id(0)

        @pl.when(step == 0)
        def _():
            cross = ordered(core_ref[0], mine_ref[...], other_ref[...])
            right = dot(inverse_ref[...], cross, 1, 0, HIGHEST)
            right_ref[...] = right
            mix_ref[...] = dot(inverse_ref[...], right, 0, 0, HIGHEST)

        approx = dot(left_ref[...], mix_ref[...], 0, 0, HIGHEST)
        for part, merged_ref in enumerate(merged_refs):

            @pl.when(step // per_part == part)
            def _():
                error_ref[...] = (merged_ref[...] - approx).astype(BF16)

    def part_spec(part):
        return pl.BlockSpec(
            (block, COLUMNS), lambda i: (jnp.clip(i - part * per_part, 0, per_part - 1), 0)
        )

    return pl.pallas_call(
        body,
        grid=(steps,),
        in_specs=[
            pl.BlockSpec(memory_space=pltpu.SMEM),
            whole(mine),
            whole(other),
            whole(inverse),
            pl.BlockSpec((RANK, block), lambda i: (0, i)),
        ]
        + [part_spec(part) for part in range(len(merged_parts))],
        out_specs=[
            pl.BlockSpec((block, COLUMNS), lambda i: (i, 0)),
            pl.BlockSpec((RANK, COLUMNS), lambda i: (0, 0)),
        ],
        out_shape=[
            jax.ShapeDtypeStruct((features, COLUMNS), BF16),
            jax.ShapeDtypeStruct((RANK, COLUMNS), F32),
        ],
        scratch_shapes=[pltpu.VMEM((RANK, COLUMNS), F32)],
        compiler_params=VMEM,
        cost_estimate=cost(12 * features * COLUMNS * RANK, 6 * features * COLUMNS),
        name="finish",
    )(core, mine, other, inverse, left, *merged_parts)


def input_gradient(grads, weights, block):
    features = weights[0].shape[0]
    count = len(grads)

    def body(*refs):
        total = None
        for grad_ref, weight_ref in zip(refs[:count], refs[count:-1]):
            term = dot(grad_ref[...], weight_ref[...], 1, 1)
            total = term if total is None else total + term
        refs[-1][...] = total.astype(BF16)

    return pl.pallas_call(
        body,
        grid=(features // block,),
        in_specs=[whole(grad) for grad in grads]
        + [pl.BlockSpec((block, COLUMNS), lambda i: (i, 0)) for _ in weights],
        out_specs=pl.BlockSpec((PART, block), lambda i: (0, i)),
        out_shape=jax.ShapeDtypeStruct((PART, features), BF16),
        compiler_params=VMEM,
        cost_estimate=cost(2 * PART * features * 1024, 12 * features * COLUMNS),
        name="input_gradient",
    )(*grads, *weights)


def opposite_halves(from_before, from_after):
    half = from_before.shape[0] // 2
    return (
        shift(from_before[:half], "tensor", 4, 1),
        shift(from_after[half:], "tensor", 4, -1),
    )


def shards(layer_input, output_grad, query_weight, error_buffer, right_prev):
    core = lax.axis_index("c")
    place = lax.axis_index("tensor")
    error = error_buffer[0]
    core_word = core.astype(jnp.int32).reshape(1)

    grads = lax.dynamic_slice_in_dim(
        jnp.concatenate([output_grad, output_grad], 0), place * PART, SEQ, 0
    )

    cut = FEATURES // 2
    merged_parts, left_parts = [], []
    pieces = []
    chunks = [layer_input[:, :cut], layer_input[:, cut:]]
    near = [(shift(chunk, "tensor", 4, 1), shift(chunk, "tensor", 4, -1)) for chunk in chunks]
    for at, chunk in enumerate(chunks):
        before, after = near[at]
        far_low, far_high = opposite_halves(before, after)
        merged, left = merged_and_left(
            (chunk, after, far_low, far_high, before),
            grads,
            error[at * cut : (at + 1) * cut],
            right_prev,
            896,
        )
        merged_parts.append(merged)
        left_parts.append(left)
    left = jnp.concatenate(left_parts, 1)

    weight, _ = lax.optimization_barrier((query_weight, near[-1][0]))
    weight_before, weight_after = shift(weight, "tensor", 4, 1), shift(weight, "tensor", 4, -1)
    weight_far = jnp.concatenate(opposite_halves(weight_before, weight_after), 0)
    own_grads = [grads[:PART]] + [
        shift(grads[k * PART : (k + 1) * PART], "tensor", 4, k) for k in (1, 2, 3)
    ]

    mine = lax.dynamic_slice_in_dim(left, core * HALF, HALF, 0)
    other = lax.dynamic_slice_in_dim(left, (1 - core) * HALF, HALF, 0)
    mine = mine + shift(other, "c", 2, 1)
    blocks = mine.reshape(8, 4, 4, 896).transpose(0, 2, 1, 3).reshape(32, 4, 896)
    blocks = lax.all_to_all(blocks, PLANE, 0, 0, tiled=True)
    reduced = jnp.sum(blocks, 0) * (1 / REPLICAS)
    blocks = lax.all_to_all(jnp.broadcast_to(reduced, (32, 4, 896)), PLANE, 0, 0, tiled=True)
    mine = blocks.reshape(8, 4, 4, 896).transpose(0, 2, 1, 3).reshape(HALF, FEATURES)
    other = shift(mine, "c", 2, 1)

    left, cross, gram = products(core_word, mine, other, merged_parts, 1792)
    inverse = inverse_factor(gram)

    mine = lax.dynamic_slice_in_dim(cross, core * HALF, HALF, 0)
    other = lax.dynamic_slice_in_dim(cross, (1 - core) * HALF, HALF, 0)
    mine = (mine + shift(other, "c", 2, 1)) * (1 / REPLICAS)
    for axis, size in (("x", 4), ("z", 8)):
        copies = jnp.broadcast_to(mine[None], (size, HALF, COLUMNS))
        mine = jnp.sum(lax.all_to_all(copies, axis, 0, 0, tiled=True), 0)
    other = shift(mine, "c", 2, 1)

    error_next, right = finish(core_word, mine, other, inverse, left, merged_parts, 896)
    input_grad = input_gradient(
        own_grads, [query_weight, weight_before, weight_far, weight_after], 896
    )
    return input_grad, right.T, error_next[None]


def solution(mesh):
    split = Mesh(mesh.devices.reshape(8, 4, 2, 4), ("z", "x", "c", "tensor"))
    dp = ("z", "x", "c")
    in_specs = (
        P((*dp, "tensor"), None),
        P(dp, "tensor"),
        P(None, "tensor"),
        P(dp, None, "tensor"),
        P("tensor", None),
    )
    out_specs = (P((*dp, "tensor"), None), P("tensor", None), P(dp, None, "tensor"))
    return jax.shard_map(
        shards, mesh=split, in_specs=in_specs, out_specs=out_specs, check_vma=False
    )
```

```python
import jax
import jax.numpy as jnp
from jax import lax
from jax.experimental import pallas as pl
from jax.experimental.pallas import tpu as pltpu
from jax.sharding import Mesh, PartitionSpec as P

F32, BF16 = jnp.float32, jnp.bfloat16
HIGHEST = lax.Precision.HIGHEST
FEATURES, COLUMNS, RANK, SEQ, PART = 3584, 256, 64, 768, 192
HALF = RANK // 2
REPLICAS = 64
STEP = 896
TILES = (8, 4, 7, 4, 128)
HALF_FEATURES, FIRST = FEATURES // 2, 1024
PLANE = ("z", "x")
SMALL = pl.CostEstimate(flops=1000, bytes_accessed=1000, transcendentals=0)
VMEM = pltpu.CompilerParams(vmem_limit_bytes=40 * 2**20)
ALL_VMEM = pltpu.CompilerParams(vmem_limit_bytes=60 * 2**20)


def dot(a, b, dim_a, dim_b, precision=None):
    return lax.dot_general(
        a, b, (((dim_a,), (dim_b,)), ((), ())), precision=precision, preferred_element_type=F32
    )


def whole(array):
    return pl.BlockSpec(array.shape, lambda i: (0,) * array.ndim)


def shift(value, axis, size, by):
    return lax.ppermute(value, axis, [(at, (at + by) % size) for at in range(size)])


def split(value):
    high = value.astype(BF16)
    rest = value - high.astype(F32)
    middle = rest.astype(BF16)
    return high, middle, (rest - middle.astype(F32)).astype(BF16)


def stacked_dot(a, b, dim_b):
    rows = a.shape[0]
    stack = jnp.concatenate(split(a), 0)
    high, middle, low = split(b)
    first = dot(stack, high, 1, dim_b)
    second = dot(stack[: 2 * rows], middle, 1, dim_b)
    third = dot(stack[:rows], low, 1, dim_b)
    small = first[2 * rows :] + second[rows:] + third
    return first[:rows] + (first[rows : 2 * rows] + second[:rows] + small)


def merged_and_left(core, pieces, grads, error, right, offset, before):
    chunk = pieces[0].shape[1]
    first = offset // STEP
    count = len(pieces)

    def body(core_ref, *refs):
        piece_refs = refs[:count]
        grad_ref, error_ref, right_ref = refs[count : count + 3]
        merged_ref, mine_ref, other_ref = refs[-3:]
        tokens = jnp.concatenate([ref[...] for ref in piece_refs], 0)
        transposed = dot(grad_ref[...], tokens, 0, 0)
        merged = transposed.T + error_ref[...].astype(F32)
        merged_ref[...] = merged
        left = stacked_dot(right_ref[...], merged, 1)
        low, high = left[:HALF], left[HALF:]
        is_first = core_ref[0] == 0
        mine, other = jnp.where(is_first, low, high), jnp.where(is_first, high, low)
        for row in range(8):
            for lane in range(7):
                tile = slice(row * 4, row * 4 + 4), slice(lane * 128, lane * 128 + 128)
                mine_ref[row, 0, lane] = mine[tile]
                other_ref[row, 0, lane] = other[tile]

    aliased = [] if before is None else list(before)
    tiles = pl.BlockSpec((8, 1, 7, 4, 128), lambda i: (0, first + i, 0, 0, 0))
    return pl.pallas_call(
        body,
        grid=(chunk // STEP,),
        in_specs=[pl.BlockSpec(memory_space=pltpu.SMEM)]
        + [pl.BlockSpec((piece.shape[0], STEP), lambda i: (0, i)) for piece in pieces]
        + [whole(grads), pl.BlockSpec((STEP, COLUMNS), lambda i: (first + i, 0)), whole(right)]
        + [pl.BlockSpec(memory_space=pl.ANY) for _ in aliased],
        out_specs=[pl.BlockSpec((STEP, COLUMNS), lambda i: (first + i, 0)), tiles, tiles],
        out_shape=[
            jax.ShapeDtypeStruct((FEATURES, COLUMNS), F32),
            jax.ShapeDtypeStruct(TILES, F32),
            jax.ShapeDtypeStruct(TILES, F32),
        ],
        input_output_aliases={4 + count + at: at for at in range(len(aliased))},
        compiler_params=ALL_VMEM,
        cost_estimate=SMALL,
        name="merged_and_left",
    )(core, *pieces, grads, error, right, *aliased)


def ordered(core, mine, other):
    first = core == 0
    return jnp.concatenate([jnp.where(first, mine, other), jnp.where(first, other, mine)], 0)


def products(core, mine, other, merged):
    def body(core_ref, mine_ref, other_ref, merged_ref, left_ref, cross_ref, gram_ref):
        @pl.when(pl.program_id(0) == 0)
        def _():
            cross_ref[...] = jnp.zeros_like(cross_ref)
            gram_ref[...] = jnp.zeros_like(gram_ref)

        def rows(ref):
            return jnp.concatenate(
                [jnp.concatenate([ref[row, 0, lane] for lane in range(7)], 1) for row in range(8)],
                0,
            )

        left = ordered(core_ref[0], rows(mine_ref), rows(other_ref))
        left_ref[...] = left
        stack = jnp.concatenate(split(left), 0)
        squares = dot(stack, stack, 1, 1)

        def square(a, b):
            return squares[a * RANK : (a + 1) * RANK, b * RANK : (b + 1) * RANK]

        small = square(0, 2) + square(2, 0) + square(1, 1)
        gram_ref[...] += square(0, 0) + (square(0, 1) + square(1, 0) + small)
        cross_ref[...] += stacked_dot(left, merged_ref[...], 0)

    tiles = pl.BlockSpec((8, 1, 7, 4, 128), lambda i: (0, i, 0, 0, 0))
    return pl.pallas_call(
        body,
        grid=(FEATURES // STEP,),
        in_specs=[
            pl.BlockSpec(memory_space=pltpu.SMEM),
            tiles,
            tiles,
            pl.BlockSpec((STEP, COLUMNS), lambda i: (i, 0)),
        ],
        out_specs=[
            pl.BlockSpec((RANK, STEP), lambda i: (0, i)),
            pl.BlockSpec((RANK, COLUMNS), lambda i: (0, 0)),
            pl.BlockSpec((RANK, RANK), lambda i: (0, 0)),
        ],
        out_shape=[
            jax.ShapeDtypeStruct((RANK, FEATURES), F32),
            jax.ShapeDtypeStruct((RANK, COLUMNS), F32),
            jax.ShapeDtypeStruct((RANK, RANK), F32),
        ],
        compiler_params=VMEM,
        cost_estimate=SMALL,
        name="cross_and_gram",
    )(core, mine, other, merged)


def inverse_factor(gram):
    def body(gram_ref, inverse_ref):
        rows = lax.broadcasted_iota(jnp.int32, (RANK, 2 * RANK), 0)
        lanes = lax.broadcasted_iota(jnp.int32, (RANK, 2 * RANK), 1)
        work = jnp.concatenate([gram_ref[...], jnp.zeros((RANK, RANK), F32)], 1)
        work = jnp.where(lanes == rows + RANK, 1.0, work)
        for at in range(RANK):
            pivot_row = work[at : at + 1, :]
            factor = work[:, at : at + 1] * (1.0 / pivot_row[:, at : at + 1])
            work = jnp.where(rows > at, work - factor * pivot_row, work)
        pivots = jnp.sum(jnp.where(lanes == rows, work, 0.0), 1, keepdims=True)
        inverse_ref[...] = work[:, RANK:] * (1.0 / jnp.sqrt(pivots))

    return pl.pallas_call(
        body,
        out_shape=jax.ShapeDtypeStruct((RANK, RANK), F32),
        cost_estimate=SMALL,
        name="inverse_factor",
    )(gram)


def orthonormal(inverse, left, block):
    def body(inverse_ref, left_ref, basis_ref):
        basis = stacked_dot(inverse_ref[...], left_ref[...], 0).T
        high = basis.astype(BF16)
        low = (basis - high.astype(F32)).astype(BF16)
        basis_ref[...] = jnp.concatenate([high, low], 1)

    return pl.pallas_call(
        body,
        grid=(FEATURES // block,),
        in_specs=[whole(inverse), pl.BlockSpec((RANK, block), lambda i: (0, i))],
        out_specs=pl.BlockSpec((block, 2 * RANK), lambda i: (i, 0)),
        out_shape=jax.ShapeDtypeStruct((FEATURES, 2 * RANK), BF16),
        compiler_params=VMEM,
        cost_estimate=SMALL,
        name="orthonormal",
    )(inverse, left)


def finish(core, mine, other, inverse, basis, merged, block):
    def body(core_ref, mine_ref, other_ref, inverse_ref, basis_ref, merged_ref, *refs):
        error_ref, right_ref, parts_ref = refs

        @pl.when(pl.program_id(0) == 0)
        def _():
            cross = ordered(core_ref[0], mine_ref[...], other_ref[...])
            right = dot(inverse_ref[...], cross, 1, 0, HIGHEST)
            right_ref[...] = right
            high = right.astype(BF16)
            low = (right - high.astype(F32)).astype(BF16)
            parts_ref[...] = jnp.concatenate([high, high, low, low], 0)

        both = jnp.concatenate([basis_ref[...], basis_ref[...]], 1)
        approx = dot(both, parts_ref[...], 1, 0)
        error_ref[...] = (merged_ref[...] - approx).astype(BF16)

    rows = pl.BlockSpec((block, COLUMNS), lambda i: (i, 0))
    return pl.pallas_call(
        body,
        grid=(FEATURES // block,),
        in_specs=[
            pl.BlockSpec(memory_space=pltpu.SMEM),
            whole(mine),
            whole(other),
            whole(inverse),
            pl.BlockSpec((block, 2 * RANK), lambda i: (i, 0)),
            rows,
        ],
        out_specs=[rows, pl.BlockSpec((RANK, COLUMNS), lambda i: (0, 0))],
        out_shape=[
            jax.ShapeDtypeStruct((FEATURES, COLUMNS), BF16),
            jax.ShapeDtypeStruct((RANK, COLUMNS), F32),
        ],
        scratch_shapes=[pltpu.VMEM((4 * RANK, COLUMNS), BF16)],
        compiler_params=VMEM,
        cost_estimate=SMALL,
        name="finish",
    )(core, mine, other, inverse, basis, merged)


def input_gradient(core, grads, weight, mine, other):
    def body(core_ref, grad_ref, weight_ref, *refs):
        *parcel_refs, out_ref = refs
        before_high, far, after_high = parcel_refs[1], parcel_refs[4], parcel_refs[3]
        blocks = [
            grad_ref[...],
            before_high[HALF_FEATURES - FIRST :, :],
            far[HALF_FEATURES:, :],
            after_high[HALF_FEATURES - FIRST :, :],
        ]
        for side in range(2):
            half = core_ref[0] if side == 0 else 1 - core_ref[0]
            before_low, before_high, after_low, after_high, far = parcel_refs[
                5 * side : 5 * side + 5
            ]
            for first, count, near in (
                (0, FIRST, (before_low, after_low)),
                (FIRST, HALF_FEATURES - FIRST, (before_high, after_high)),
            ):
                start = pl.multiple_of(half * HALF_FEATURES + first, 128)
                total = dot(blocks[0], weight_ref[pl.ds(start, count), :], 1, 1)
                total = total + dot(blocks[1], near[0][:count, :], 1, 1)
                total = total + dot(blocks[2], far[first : first + count, :], 1, 1)
                total = total + dot(blocks[3], near[1][:count, :], 1, 1)
                out_ref[:, pl.ds(start, count)] = total.astype(BF16)

    vmem = pl.BlockSpec(memory_space=pltpu.VMEM)
    return pl.pallas_call(
        body,
        in_specs=[pl.BlockSpec(memory_space=pltpu.SMEM)] + [vmem] * 12,
        out_specs=vmem,
        out_shape=jax.ShapeDtypeStruct((PART, FEATURES), BF16),
        compiler_params=VMEM,
        cost_estimate=SMALL,
        name="input_gradient",
    )(core, grads, weight, *mine, *other)


def both_ways(value):
    return shift(value, "tensor", 4, 1), shift(value, "tensor", 4, -1)


def shards(layer_input, output_grad, query_weight, error_buffer, right_prev):
    core = lax.axis_index("c")
    place = lax.axis_index("tensor")
    error = error_buffer[0]
    core_word = core.astype(jnp.int32).reshape(1)

    grads = lax.dynamic_slice_in_dim(
        jnp.concatenate([output_grad, output_grad], 0), place * PART, SEQ, 0
    )
    right_rows = right_prev.T

    cut = FEATURES // 2
    chunks = [layer_input[:, :cut], layer_input[:, cut:]]
    near = [both_ways(chunk) for chunk in chunks]
    far = [
        (shift(before[:96], "tensor", 4, 1), shift(after[96:], "tensor", 4, -1))
        for before, after in near
    ]
    state = None
    for at, chunk in enumerate(chunks):
        before, after = near[at]
        pieces = (chunk, after, *far[at], before)
        state = merged_and_left(core_word, pieces, grads, error, right_rows, at * cut, state)
    merged, mine, other = state

    half = lax.dynamic_slice_in_dim(query_weight, core * HALF_FEATURES, HALF_FEATURES, 0)
    low, high = half[:FIRST], half[FIRST:]
    before, far_parcel, after = (
        jnp.concatenate([rows, grads[k * PART : (k + 1) * PART]], 0)
        for rows, k in ((high, 1), (half, 2), (high, 3))
    )
    low, before, far_parcel, after = lax.optimization_barrier(
        (low, before, far_parcel, after, near[1][0])
    )[:4]
    lows = both_ways(low)

    total = (mine + shift(other, "c", 2, 1)).reshape(32, 7, 4, 128)
    blocks = lax.all_to_all(total, PLANE, 0, 0, tiled=True)
    reduced = jnp.sum(blocks, 0) * (1 / REPLICAS)
    reduced, *lows = lax.optimization_barrier((reduced, *lows))
    parcels = (
        lows[0],
        shift(before, "tensor", 4, 1),
        lows[1],
        shift(after, "tensor", 4, -1),
        shift(far_parcel, "tensor", 4, 2),
    )
    copies = jnp.broadcast_to(reduced, (32, 7, 4, 128))
    mine = lax.all_to_all(copies, PLANE, 0, 0, tiled=True).reshape(TILES)
    other = shift(mine, "c", 2, 1)

    left, cross, gram = products(core_word, mine, other, merged)
    inverse = inverse_factor(gram)

    mine = lax.dynamic_slice_in_dim(cross, core * HALF, HALF, 0)
    other = lax.dynamic_slice_in_dim(cross, (1 - core) * HALF, HALF, 0)
    mine = (mine + shift(other, "c", 2, 1)) * (1 / REPLICAS)
    copies = jnp.broadcast_to(mine[None], (4, HALF, COLUMNS))
    mine = jnp.sum(lax.all_to_all(copies, "x", 0, 0, tiled=True), 0)

    mine, inverse, *parcels = lax.optimization_barrier((mine, inverse, *parcels))
    other_parcels = [shift(parcel, "c", 2, 1) for parcel in parcels]
    basis = orthonormal(inverse, left, 896)
    input_grad = input_gradient(core_word, grads[:PART], query_weight, parcels, other_parcels)

    copies = jnp.broadcast_to(mine[None], (8, HALF, COLUMNS))
    blocks = lax.all_to_all(copies, "z", 0, 0, tiled=True)
    blocks, basis, input_grad = lax.optimization_barrier((blocks, basis, input_grad))
    mine = jnp.sum(blocks, 0)
    other = shift(mine, "c", 2, 1)

    error_next, right = finish(core_word, mine, other, inverse, basis, merged, 896)
    return input_grad, right.T, error_next[None]


def solution(mesh):
    split = Mesh(mesh.devices.reshape(8, 4, 2, 4), ("z", "x", "c", "tensor"))
    dp = ("z", "x", "c")
    in_specs = (
        P((*dp, "tensor"), None),
        P(dp, "tensor"),
        P(None, "tensor"),
        P(dp, None, "tensor"),
        P("tensor", None),
    )
    out_specs = (P((*dp, "tensor"), None), P("tensor", None), P(dp, None, "tensor"))
    return jax.shard_map(
        shards, mesh=split, in_specs=in_specs, out_specs=out_specs, check_vma=False
    )
```

```python
import jax
import jax.numpy as jnp
from jax import lax
from jax.experimental import pallas as pl
from jax.experimental.pallas import tpu as pltpu
from jax.sharding import Mesh, PartitionSpec as P

F32, BF16 = jnp.float32, jnp.bfloat16
HIGHEST = lax.Precision.HIGHEST
FEATURES, COLUMNS, RANK, SEQ, PART = 3584, 256, 64, 768, 192
HALF = RANK // 2
REPLICAS = 64
STEP = 896
TILES = (8, 4, 7, 4, 128)
HALF_FEATURES = FEATURES // 2
PIVOTS = 8
PLANE = ("z", "x")
SMALL = pl.CostEstimate(flops=1000, bytes_accessed=1000, transcendentals=0)
VMEM = pltpu.CompilerParams(vmem_limit_bytes=40 * 2**20)
ALL_VMEM = pltpu.CompilerParams(vmem_limit_bytes=60 * 2**20)


def dot(a, b, dim_a, dim_b, precision=None):
    return lax.dot_general(
        a, b, (((dim_a,), (dim_b,)), ((), ())), precision=precision, preferred_element_type=F32
    )


def whole(array):
    return pl.BlockSpec(array.shape, lambda i: (0,) * array.ndim)


def shift(value, axis, size, by):
    return lax.ppermute(value, axis, [(at, (at + by) % size) for at in range(size)])


def split(value):
    high = value.astype(BF16)
    rest = value - high.astype(F32)
    middle = rest.astype(BF16)
    return high, middle, (rest - middle.astype(F32)).astype(BF16)


def stacked_dot(a, b, dim_b):
    rows = a.shape[0]
    stack = jnp.concatenate(split(a), 0)
    high, middle, low = split(b)
    first = dot(stack, high, 1, dim_b)
    second = dot(stack[: 2 * rows], middle, 1, dim_b)
    third = dot(stack[:rows], low, 1, dim_b)
    small = first[2 * rows :] + second[rows:] + third
    return first[:rows] + (first[rows : 2 * rows] + second[:rows] + small)


def merged_and_left(core, pieces, grads, error, right):
    count = len(pieces)

    def body(core_ref, *refs):
        piece_refs = refs[:count]
        grad_ref, error_ref, right_ref = refs[count : count + 3]
        merged_ref, mine_ref, other_ref = refs[-3:]
        tokens = jnp.concatenate([ref[...] for ref in piece_refs], 0)
        transposed = dot(grad_ref[...], tokens, 0, 0)
        merged = transposed.T + error_ref[...].astype(F32)
        merged_ref[...] = merged
        left = stacked_dot(right_ref[...], merged, 1)
        low, high = left[:HALF], left[HALF:]
        is_first = core_ref[0] == 0
        mine, other = jnp.where(is_first, low, high), jnp.where(is_first, high, low)
        for row in range(8):
            for lane in range(7):
                tile = slice(row * 4, row * 4 + 4), slice(lane * 128, lane * 128 + 128)
                mine_ref[row, 0, lane] = mine[tile]
                other_ref[row, 0, lane] = other[tile]

    tiles = pl.BlockSpec((8, 1, 7, 4, 128), lambda i: (0, i, 0, 0, 0))
    return pl.pallas_call(
        body,
        grid=(FEATURES // STEP,),
        in_specs=[pl.BlockSpec(memory_space=pltpu.SMEM)]
        + [pl.BlockSpec((piece.shape[0], STEP), lambda i: (0, i)) for piece in pieces]
        + [whole(grads), pl.BlockSpec((STEP, COLUMNS), lambda i: (i, 0)), whole(right)],
        out_specs=[pl.BlockSpec((STEP, COLUMNS), lambda i: (i, 0)), tiles, tiles],
        out_shape=[
            jax.ShapeDtypeStruct((FEATURES, COLUMNS), F32),
            jax.ShapeDtypeStruct(TILES, F32),
            jax.ShapeDtypeStruct(TILES, F32),
        ],
        compiler_params=ALL_VMEM,
        cost_estimate=SMALL,
        name="merged_and_left",
    )(core, *pieces, grads, error, right)


def ordered(core, mine, other):
    first = core == 0
    return jnp.concatenate([jnp.where(first, mine, other), jnp.where(first, other, mine)], 0)


def products(core, mine, other, merged):
    def body(core_ref, mine_ref, other_ref, merged_ref, left_ref, cross_ref, gram_ref):
        @pl.when(pl.program_id(0) == 0)
        def _():
            cross_ref[...] = jnp.zeros_like(cross_ref)
            gram_ref[...] = jnp.zeros_like(gram_ref)

        def rows(ref):
            return jnp.concatenate(
                [jnp.concatenate([ref[row, 0, lane] for lane in range(7)], 1) for row in range(8)],
                0,
            )

        left = ordered(core_ref[0], rows(mine_ref), rows(other_ref))
        left_ref[...] = left
        stack = jnp.concatenate(split(left), 0)
        squares = dot(stack, stack, 1, 1)

        def square(a, b):
            return squares[a * RANK : (a + 1) * RANK, b * RANK : (b + 1) * RANK]

        small = square(0, 2) + square(2, 0) + square(1, 1)
        gram_ref[...] += square(0, 0) + (square(0, 1) + square(1, 0) + small)
        cross_ref[...] += stacked_dot(left, merged_ref[...], 0)

    tiles = pl.BlockSpec((8, 1, 7, 4, 128), lambda i: (0, i, 0, 0, 0))
    return pl.pallas_call(
        body,
        grid=(FEATURES // STEP,),
        in_specs=[
            pl.BlockSpec(memory_space=pltpu.SMEM),
            tiles,
            tiles,
            pl.BlockSpec((STEP, COLUMNS), lambda i: (i, 0)),
        ],
        out_specs=[
            pl.BlockSpec((RANK, STEP), lambda i: (0, i)),
            pl.BlockSpec((RANK, COLUMNS), lambda i: (0, 0)),
            pl.BlockSpec((RANK, RANK), lambda i: (0, 0)),
        ],
        out_shape=[
            jax.ShapeDtypeStruct((RANK, FEATURES), F32),
            jax.ShapeDtypeStruct((RANK, COLUMNS), F32),
            jax.ShapeDtypeStruct((RANK, RANK), F32),
        ],
        compiler_params=VMEM,
        cost_estimate=SMALL,
        name="cross_and_gram",
    )(core, mine, other, merged)


def inverse_factor(gram):
    def body(gram_ref, inverse_ref):
        shape = (PIVOTS, 2 * RANK)
        rows = lax.broadcasted_iota(jnp.int32, (RANK, 2 * RANK), 0)
        lanes = lax.broadcasted_iota(jnp.int32, (RANK, 2 * RANK), 1)
        work = jnp.concatenate([gram_ref[...], jnp.zeros((RANK, RANK), F32)], 1)
        work = jnp.where(lanes == rows + RANK, 1.0, work)
        tiles = [work[at : at + PIVOTS] for at in range(0, RANK, PIVOTS)]
        local = lax.broadcasted_iota(jnp.int32, shape, 0)
        for at in range(len(tiles)):
            columns = [
                [
                    jnp.broadcast_to(tile[:, at * PIVOTS + k : at * PIVOTS + k + 1], shape)
                    for tile in tiles[at:]
                ]
                for k in range(PIVOTS)
            ]
            pivot_rows = [tiles[at][k : k + 1] for k in range(PIVOTS)]
            updates = [0.0] * len(tiles[at:])
            for k in range(PIVOTS):
                inverse = 1.0 / columns[k][0][k : k + 1]
                scaled = pivot_rows[k] * inverse
                for later in range(k + 1, PIVOTS):
                    pivot_rows[later] -= columns[k][0][later : later + 1] * scaled
                    factor = columns[later][0][k : k + 1] * inverse
                    columns[later] = [
                        column - done * factor
                        for column, done in zip(columns[later], columns[k])
                    ]
                updates = [update + done * scaled for update, done in zip(updates, columns[k])]
            for k in range(1, PIVOTS):
                tiles[at] = jnp.where(local == k, pivot_rows[k], tiles[at])
            for below in range(1, len(updates)):
                tiles[at + below] = tiles[at + below] - updates[below]
        work = jnp.concatenate(tiles, 0)
        pivots = jnp.sum(jnp.where(lanes == rows, work, 0.0), 1, keepdims=True)
        inverse_ref[...] = work[:, RANK:] * (1.0 / jnp.sqrt(pivots))

    return pl.pallas_call(
        body,
        out_shape=jax.ShapeDtypeStruct((RANK, RANK), F32),
        cost_estimate=SMALL,
        name="inverse_factor",
    )(gram)


def orthonormal(inverse, left, block):
    def body(inverse_ref, left_ref, basis_ref):
        basis = stacked_dot(inverse_ref[...], left_ref[...], 0).T
        high = basis.astype(BF16)
        low = (basis - high.astype(F32)).astype(BF16)
        basis_ref[...] = jnp.concatenate([high, low], 1)

    return pl.pallas_call(
        body,
        grid=(FEATURES // block,),
        in_specs=[whole(inverse), pl.BlockSpec((RANK, block), lambda i: (0, i))],
        out_specs=pl.BlockSpec((block, 2 * RANK), lambda i: (i, 0)),
        out_shape=jax.ShapeDtypeStruct((FEATURES, 2 * RANK), BF16),
        compiler_params=VMEM,
        cost_estimate=SMALL,
        name="orthonormal",
    )(inverse, left)


def finish(core, mine, other, inverse, basis, merged, block):
    def body(core_ref, mine_ref, other_ref, inverse_ref, basis_ref, merged_ref, *refs):
        error_ref, right_ref, parts_ref = refs

        @pl.when(pl.program_id(0) == 0)
        def _():
            cross = ordered(core_ref[0], mine_ref[...], other_ref[...])
            right = dot(inverse_ref[...], cross, 1, 0, HIGHEST)
            right_ref[...] = right
            high = right.astype(BF16)
            low = (right - high.astype(F32)).astype(BF16)
            parts_ref[...] = jnp.concatenate([high, high, low, low], 0)

        both = jnp.concatenate([basis_ref[...], basis_ref[...]], 1)
        approx = dot(both, parts_ref[...], 1, 0)
        error_ref[...] = (merged_ref[...] - approx).astype(BF16)

    rows = pl.BlockSpec((block, COLUMNS), lambda i: (i, 0))
    return pl.pallas_call(
        body,
        grid=(FEATURES // block,),
        in_specs=[
            pl.BlockSpec(memory_space=pltpu.SMEM),
            whole(mine),
            whole(other),
            whole(inverse),
            pl.BlockSpec((block, 2 * RANK), lambda i: (i, 0)),
            rows,
        ],
        out_specs=[rows, pl.BlockSpec((RANK, COLUMNS), lambda i: (0, 0))],
        out_shape=[
            jax.ShapeDtypeStruct((FEATURES, COLUMNS), BF16),
            jax.ShapeDtypeStruct((RANK, COLUMNS), F32),
        ],
        scratch_shapes=[pltpu.VMEM((4 * RANK, COLUMNS), BF16)],
        compiler_params=VMEM,
        cost_estimate=SMALL,
        name="finish",
    )(core, mine, other, inverse, basis, merged)


def input_gradient(core, grads, weight, mine, other):
    def body(core_ref, grad_ref, weight_ref, *refs):
        *parcel_refs, out_ref = refs

        def fill(halves):
            for first in range(0, HALF_FEATURES, 896):
                rows = slice(first, first + 896)
                total = dot(grad_ref[...], weight_ref[rows, :], 1, 1)
                for sent, weights in zip(parcel_refs, halves):
                    total = total + dot(sent[HALF_FEATURES:, :], weights[rows, :], 1, 1)
                out_ref[:, rows] = total.astype(BF16)

        @pl.when(pl.program_id(0) == 0)
        def _():
            fill(parcel_refs[:3])

        @pl.when(pl.program_id(0) == 1)
        def _():
            fill(parcel_refs[3:])

    def half(side, core_ref):
        return side + core_ref[0] * (1 - 2 * side)

    vmem = pl.BlockSpec(memory_space=pltpu.VMEM)
    return pl.pallas_call(
        body,
        grid_spec=pltpu.PrefetchScalarGridSpec(
            num_scalar_prefetch=1,
            grid=(2,),
            in_specs=[
                pl.BlockSpec((PART, COLUMNS), lambda side, core_ref: (0, 0)),
                pl.BlockSpec(
                    (HALF_FEATURES, COLUMNS), lambda side, core_ref: (half(side, core_ref), 0)
                ),
            ]
            + [vmem] * 6,
            out_specs=pl.BlockSpec(
                (PART, HALF_FEATURES), lambda side, core_ref: (0, half(side, core_ref))
            ),
        ),
        out_shape=jax.ShapeDtypeStruct((PART, FEATURES), BF16),
        compiler_params=VMEM,
        cost_estimate=SMALL,
        name="input_gradient",
    )(core, grads, weight, *mine, *other)


def summed_copies(blocks, count):
    def body(blocks_ref, copies_ref):
        mean = jnp.sum(blocks_ref[...], 0) * (1 / REPLICAS)
        copies_ref[...] = jnp.broadcast_to(mean[None], copies_ref.shape)

    return pl.pallas_call(
        body,
        out_shape=jax.ShapeDtypeStruct((count, *blocks.shape[1:]), F32),
        compiler_params=VMEM,
        cost_estimate=SMALL,
        name="summed_copies",
    )(blocks)


def both_ways(value):
    return shift(value, "tensor", 4, 1), shift(value, "tensor", 4, -1)


def shards(layer_input, output_grad, query_weight, error_buffer, right_prev):
    core = lax.axis_index("c")
    place = lax.axis_index("tensor")
    error = error_buffer[0]
    core_word = core.astype(jnp.int32).reshape(1)

    grads = lax.dynamic_slice_in_dim(
        jnp.concatenate([output_grad, output_grad], 0), place * PART, SEQ, 0
    )
    right_rows = right_prev.T

    low, high = layer_input[: PART // 2], layer_input[PART // 2 :]
    before_low, after_high = shift(low, "tensor", 4, 1), shift(high, "tensor", 4, -1)
    before_high, after_low = shift(high, "tensor", 4, 1), shift(low, "tensor", 4, -1)
    far_low, far_high = shift(before_low, "tensor", 4, 1), shift(after_high, "tensor", 4, -1)
    pieces = (layer_input, after_low, after_high, far_low, far_high, before_low, before_high)
    merged, mine, other = merged_and_left(core_word, pieces, grads, error, right_rows)

    half = lax.dynamic_slice_in_dim(query_weight, core * HALF_FEATURES, HALF_FEATURES, 0)
    parcels = [
        jnp.concatenate([half, grads[k * PART : (k + 1) * PART]], 0) for k in (1, 2, 3)
    ]
    parcels = lax.optimization_barrier((*parcels, before_high))[:3]
    before, after = shift(parcels[0], "tensor", 4, 1), shift(parcels[2], "tensor", 4, -1)

    total = (mine + shift(other, "c", 2, 1)).reshape(32, 7, 4, 128)
    blocks = lax.all_to_all(total, PLANE, 0, 0, tiled=True)
    blocks, before, after = lax.optimization_barrier((blocks, before, after))
    parcels = (before, shift(parcels[1], "tensor", 4, 2), after)
    copies = summed_copies(blocks, 32)
    mine = lax.all_to_all(copies, PLANE, 0, 0, tiled=True).reshape(TILES)
    other = shift(mine, "c", 2, 1)

    left, cross, gram = products(core_word, mine, other, merged)
    inverse = inverse_factor(gram)

    mine = lax.dynamic_slice_in_dim(cross, core * HALF, HALF, 0)
    other = lax.dynamic_slice_in_dim(cross, (1 - core) * HALF, HALF, 0)
    mine = (mine + shift(other, "c", 2, 1)) * (1 / REPLICAS)
    copies = jnp.broadcast_to(mine[None], (4, HALF, COLUMNS))
    mine = jnp.sum(lax.all_to_all(copies, "x", 0, 0, tiled=True), 0)

    mine, inverse, *parcels = lax.optimization_barrier((mine, inverse, *parcels))
    other_parcels = [shift(parcel, "c", 2, 1) for parcel in parcels]
    basis = orthonormal(inverse, left, 896)
    input_grad = input_gradient(core_word, grads[:PART], query_weight, parcels, other_parcels)

    copies = jnp.broadcast_to(mine[None], (8, HALF, COLUMNS))
    blocks = lax.all_to_all(copies, "z", 0, 0, tiled=True)
    blocks, basis, input_grad = lax.optimization_barrier((blocks, basis, input_grad))
    mine = jnp.sum(blocks, 0)
    other = shift(mine, "c", 2, 1)

    error_next, right = finish(core_word, mine, other, inverse, basis, merged, 896)
    return input_grad, right.T, error_next[None]


def solution(mesh):
    split = Mesh(mesh.devices.reshape(8, 4, 2, 4), ("z", "x", "c", "tensor"))
    dp = ("z", "x", "c")
    in_specs = (
        P((*dp, "tensor"), None),
        P(dp, "tensor"),
        P(None, "tensor"),
        P(dp, None, "tensor"),
        P("tensor", None),
    )
    out_specs = (P((*dp, "tensor"), None), P("tensor", None), P(dp, None, "tensor"))
    return jax.shard_map(
        shards, mesh=split, in_specs=in_specs, out_specs=out_specs, check_vma=False
    )
```

```python
import jax
import jax.numpy as jnp
from jax import lax
from jax.experimental import pallas as pl
from jax.experimental.pallas import tpu as pltpu
from jax.sharding import Mesh, PartitionSpec as P

F32, BF16 = jnp.float32, jnp.bfloat16
HIGHEST = lax.Precision.HIGHEST
FEATURES, COLUMNS, RANK, SEQ, PART = 3584, 256, 64, 768, 192
HALF = RANK // 2
REPLICAS = 64
STEP = 896
TILES = (8, 4, 7, 4, 128)
HALF_FEATURES = FEATURES // 2
PIVOTS = 8
PLANE = ("z", "x")
SMALL = pl.CostEstimate(flops=1000, bytes_accessed=1000, transcendentals=0)
VMEM = pltpu.CompilerParams(vmem_limit_bytes=40 * 2**20)
ALL_VMEM = pltpu.CompilerParams(vmem_limit_bytes=60 * 2**20)


def dot(a, b, dim_a, dim_b, precision=None):
    return lax.dot_general(
        a, b, (((dim_a,), (dim_b,)), ((), ())), precision=precision, preferred_element_type=F32
    )


def whole(array):
    return pl.BlockSpec(array.shape, lambda i: (0,) * array.ndim)


def shift(value, axis, size, by):
    return lax.ppermute(value, axis, [(at, (at + by) % size) for at in range(size)])


def split(value):
    high = value.astype(BF16)
    rest = value - high.astype(F32)
    middle = rest.astype(BF16)
    return high, middle, (rest - middle.astype(F32)).astype(BF16)


def stacked_dot(a, b, dim_b):
    rows = a.shape[0]
    stack = jnp.concatenate(split(a), 0)
    high, middle, low = split(b)
    first = dot(stack, high, 1, dim_b)
    second = dot(stack[: 2 * rows], middle, 1, dim_b)
    third = dot(stack[:rows], low, 1, dim_b)
    small = first[2 * rows :] + second[rows:] + third
    return first[:rows] + (first[rows : 2 * rows] + second[:rows] + small)


def started_merged(pieces, grads, error):
    def body(*refs):
        *piece_refs, grad_ref, error_ref, merged_ref = refs
        tokens = jnp.concatenate([ref[...] for ref in piece_refs], 0)
        near = jnp.concatenate([grad_ref[: 2 * PART], grad_ref[3 * PART :]], 0)
        merged_ref[...] = dot(near, tokens, 0, 0).T + error_ref[...].astype(F32)

    rows = pl.BlockSpec((STEP, COLUMNS), lambda i: (i, 0))
    return pl.pallas_call(
        body,
        grid=(FEATURES // STEP,),
        in_specs=[pl.BlockSpec((piece.shape[0], STEP), lambda i: (0, i)) for piece in pieces]
        + [whole(grads), rows],
        out_specs=rows,
        out_shape=jax.ShapeDtypeStruct((FEATURES, COLUMNS), F32),
        compiler_params=VMEM,
        cost_estimate=SMALL,
        name="started_merged",
    )(*pieces, grads, error)


def merged_and_left(core, far_low, far_high, grads, started, right):
    def body(core_ref, low_ref, high_ref, grad_ref, started_ref, right_ref, *refs):
        merged_ref, mine_ref, other_ref = refs
        tokens = jnp.concatenate([low_ref[...], high_ref[...]], 0)
        far = dot(grad_ref[2 * PART : 3 * PART], tokens, 0, 0)
        merged = far.T + started_ref[...]
        merged_ref[...] = merged
        left = stacked_dot(right_ref[...], merged, 1)
        low, high = left[:HALF], left[HALF:]
        is_first = core_ref[0] == 0
        mine, other = jnp.where(is_first, low, high), jnp.where(is_first, high, low)
        for row in range(8):
            for lane in range(7):
                tile = slice(row * 4, row * 4 + 4), slice(lane * 128, lane * 128 + 128)
                mine_ref[row, 0, lane] = mine[tile]
                other_ref[row, 0, lane] = other[tile]

    rows = pl.BlockSpec((STEP, COLUMNS), lambda i: (i, 0))
    columns = pl.BlockSpec((PART // 2, STEP), lambda i: (0, i))
    tiles = pl.BlockSpec((8, 1, 7, 4, 128), lambda i: (0, i, 0, 0, 0))
    return pl.pallas_call(
        body,
        grid=(FEATURES // STEP,),
        in_specs=[pl.BlockSpec(memory_space=pltpu.SMEM), columns, columns]
        + [whole(grads), rows, whole(right)],
        out_specs=[rows, tiles, tiles],
        out_shape=[
            jax.ShapeDtypeStruct((FEATURES, COLUMNS), F32),
            jax.ShapeDtypeStruct(TILES, F32),
            jax.ShapeDtypeStruct(TILES, F32),
        ],
        compiler_params=VMEM,
        cost_estimate=SMALL,
        name="merged_and_left",
    )(core, far_low, far_high, grads, started, right)


def ordered(core, mine, other):
    first = core == 0
    return jnp.concatenate([jnp.where(first, mine, other), jnp.where(first, other, mine)], 0)


def products(core, mine, other, merged):
    def body(core_ref, mine_ref, other_ref, merged_ref, left_ref, cross_ref, gram_ref):
        @pl.when(pl.program_id(0) == 0)
        def _():
            cross_ref[...] = jnp.zeros_like(cross_ref)
            gram_ref[...] = jnp.zeros_like(gram_ref)

        def rows(ref):
            return jnp.concatenate(
                [jnp.concatenate([ref[row, 0, lane] for lane in range(7)], 1) for row in range(8)],
                0,
            )

        left = ordered(core_ref[0], rows(mine_ref), rows(other_ref))
        left_ref[...] = left
        stack = jnp.concatenate(split(left), 0)
        squares = dot(stack, stack, 1, 1)

        def square(a, b):
            return squares[a * RANK : (a + 1) * RANK, b * RANK : (b + 1) * RANK]

        small = square(0, 2) + square(2, 0) + square(1, 1)
        gram_ref[...] += square(0, 0) + (square(0, 1) + square(1, 0) + small)
        cross_ref[...] += stacked_dot(left, merged_ref[...], 0)

    tiles = pl.BlockSpec((8, 1, 7, 4, 128), lambda i: (0, i, 0, 0, 0))
    return pl.pallas_call(
        body,
        grid=(FEATURES // STEP,),
        in_specs=[
            pl.BlockSpec(memory_space=pltpu.SMEM),
            tiles,
            tiles,
            pl.BlockSpec((STEP, COLUMNS), lambda i: (i, 0)),
        ],
        out_specs=[
            pl.BlockSpec((RANK, STEP), lambda i: (0, i)),
            pl.BlockSpec((RANK, COLUMNS), lambda i: (0, 0)),
            pl.BlockSpec((RANK, RANK), lambda i: (0, 0)),
        ],
        out_shape=[
            jax.ShapeDtypeStruct((RANK, FEATURES), F32),
            jax.ShapeDtypeStruct((RANK, COLUMNS), F32),
            jax.ShapeDtypeStruct((RANK, RANK), F32),
        ],
        compiler_params=VMEM,
        cost_estimate=SMALL,
        name="cross_and_gram",
    )(core, mine, other, merged)


def inverse_factor(gram):
    def body(gram_ref, inverse_ref):
        shape = (PIVOTS, 2 * RANK)
        rows = lax.broadcasted_iota(jnp.int32, (RANK, 2 * RANK), 0)
        lanes = lax.broadcasted_iota(jnp.int32, (RANK, 2 * RANK), 1)
        work = jnp.concatenate([gram_ref[...], jnp.zeros((RANK, RANK), F32)], 1)
        work = jnp.where(lanes == rows + RANK, 1.0, work)
        tiles = [work[at : at + PIVOTS] for at in range(0, RANK, PIVOTS)]
        local = lax.broadcasted_iota(jnp.int32, shape, 0)
        for at in range(len(tiles)):
            columns = [
                [
                    jnp.broadcast_to(tile[:, at * PIVOTS + k : at * PIVOTS + k + 1], shape)
                    for tile in tiles[at:]
                ]
                for k in range(PIVOTS)
            ]
            pivot_rows = [tiles[at][k : k + 1] for k in range(PIVOTS)]
            updates = [0.0] * len(tiles[at:])
            for k in range(PIVOTS):
                inverse = 1.0 / columns[k][0][k : k + 1]
                scaled = pivot_rows[k] * inverse
                for later in range(k + 1, PIVOTS):
                    pivot_rows[later] -= columns[k][0][later : later + 1] * scaled
                    factor = columns[later][0][k : k + 1] * inverse
                    columns[later] = [
                        column - done * factor
                        for column, done in zip(columns[later], columns[k])
                    ]
                updates = [update + done * scaled for update, done in zip(updates, columns[k])]
            for k in range(1, PIVOTS):
                tiles[at] = jnp.where(local == k, pivot_rows[k], tiles[at])
            for below in range(1, len(updates)):
                tiles[at + below] = tiles[at + below] - updates[below]
        work = jnp.concatenate(tiles, 0)
        pivots = jnp.sum(jnp.where(lanes == rows, work, 0.0), 1, keepdims=True)
        inverse_ref[...] = work[:, RANK:] * (1.0 / jnp.sqrt(pivots))

    return pl.pallas_call(
        body,
        out_shape=jax.ShapeDtypeStruct((RANK, RANK), F32),
        cost_estimate=SMALL,
        name="inverse_factor",
    )(gram)


def orthonormal(inverse, left, block):
    def body(inverse_ref, left_ref, basis_ref):
        basis = stacked_dot(inverse_ref[...], left_ref[...], 0).T
        high = basis.astype(BF16)
        low = (basis - high.astype(F32)).astype(BF16)
        basis_ref[...] = jnp.concatenate([high, low], 1)

    return pl.pallas_call(
        body,
        grid=(FEATURES // block,),
        in_specs=[whole(inverse), pl.BlockSpec((RANK, block), lambda i: (0, i))],
        out_specs=pl.BlockSpec((block, 2 * RANK), lambda i: (i, 0)),
        out_shape=jax.ShapeDtypeStruct((FEATURES, 2 * RANK), BF16),
        compiler_params=VMEM,
        cost_estimate=SMALL,
        name="orthonormal",
    )(inverse, left)


def finish(core, mine, other, inverse, basis, merged, block):
    def body(core_ref, mine_ref, other_ref, inverse_ref, basis_ref, merged_ref, *refs):
        error_ref, right_ref, parts_ref = refs

        @pl.when(pl.program_id(0) == 0)
        def _():
            cross = ordered(core_ref[0], mine_ref[...], other_ref[...])
            right = dot(inverse_ref[...], cross, 1, 0, HIGHEST)
            right_ref[...] = right
            high = right.astype(BF16)
            low = (right - high.astype(F32)).astype(BF16)
            parts_ref[...] = jnp.concatenate([high, high, low, low], 0)

        both = jnp.concatenate([basis_ref[...], basis_ref[...]], 1)
        approx = dot(both, parts_ref[...], 1, 0)
        error_ref[...] = (merged_ref[...] - approx).astype(BF16)

    rows = pl.BlockSpec((block, COLUMNS), lambda i: (i, 0))
    return pl.pallas_call(
        body,
        grid=(FEATURES // block,),
        in_specs=[
            pl.BlockSpec(memory_space=pltpu.SMEM),
            whole(mine),
            whole(other),
            whole(inverse),
            pl.BlockSpec((block, 2 * RANK), lambda i: (i, 0)),
            rows,
        ],
        out_specs=[rows, pl.BlockSpec((RANK, COLUMNS), lambda i: (0, 0))],
        out_shape=[
            jax.ShapeDtypeStruct((FEATURES, COLUMNS), BF16),
            jax.ShapeDtypeStruct((RANK, COLUMNS), F32),
        ],
        scratch_shapes=[pltpu.VMEM((4 * RANK, COLUMNS), BF16)],
        compiler_params=VMEM,
        cost_estimate=SMALL,
        name="finish",
    )(core, mine, other, inverse, basis, merged)


def input_gradient(core, grads, weight, mine, other):
    def body(core_ref, grad_ref, weight_ref, *refs):
        *parcel_refs, out_ref = refs

        def fill(halves):
            for first in range(0, HALF_FEATURES, 896):
                rows = slice(first, first + 896)
                total = dot(grad_ref[...], weight_ref[rows, :], 1, 1)
                for sent, weights in zip(parcel_refs, halves):
                    total = total + dot(sent[HALF_FEATURES:, :], weights[rows, :], 1, 1)
                out_ref[:, rows] = total.astype(BF16)

        @pl.when(pl.program_id(0) == 0)
        def _():
            fill(parcel_refs[:3])

        @pl.when(pl.program_id(0) == 1)
        def _():
            fill(parcel_refs[3:])

    def half(side, core_ref):
        return side + core_ref[0] * (1 - 2 * side)

    vmem = pl.BlockSpec(memory_space=pltpu.VMEM)
    return pl.pallas_call(
        body,
        grid_spec=pltpu.PrefetchScalarGridSpec(
            num_scalar_prefetch=1,
            grid=(2,),
            in_specs=[
                pl.BlockSpec((PART, COLUMNS), lambda side, core_ref: (0, 0)),
                pl.BlockSpec(
                    (HALF_FEATURES, COLUMNS), lambda side, core_ref: (half(side, core_ref), 0)
                ),
            ]
            + [vmem] * 6,
            out_specs=pl.BlockSpec(
                (PART, HALF_FEATURES), lambda side, core_ref: (0, half(side, core_ref))
            ),
        ),
        out_shape=jax.ShapeDtypeStruct((PART, FEATURES), BF16),
        compiler_params=VMEM,
        cost_estimate=SMALL,
        name="input_gradient",
    )(core, grads, weight, *mine, *other)


def summed_copies(blocks, count):
    def body(blocks_ref, copies_ref):
        mean = jnp.sum(blocks_ref[...], 0) * (1 / REPLICAS)
        copies_ref[...] = jnp.broadcast_to(mean[None], copies_ref.shape)

    return pl.pallas_call(
        body,
        out_shape=jax.ShapeDtypeStruct((count, *blocks.shape[1:]), F32),
        compiler_params=VMEM,
        cost_estimate=SMALL,
        name="summed_copies",
    )(blocks)


def both_ways(value):
    return shift(value, "tensor", 4, 1), shift(value, "tensor", 4, -1)


def shards(layer_input, output_grad, query_weight, error_buffer, right_prev):
    core = lax.axis_index("c")
    place = lax.axis_index("tensor")
    error = error_buffer[0]
    core_word = core.astype(jnp.int32).reshape(1)

    grads = lax.dynamic_slice_in_dim(
        jnp.concatenate([output_grad, output_grad], 0), place * PART, SEQ, 0
    )
    right_rows = right_prev.T

    low, high = layer_input[: PART // 2], layer_input[PART // 2 :]
    before_low, after_high = shift(low, "tensor", 4, 1), shift(high, "tensor", 4, -1)
    before_high, after_low = shift(high, "tensor", 4, 1), shift(low, "tensor", 4, -1)
    far_low, far_high = shift(before_low, "tensor", 4, 1), shift(after_high, "tensor", 4, -1)
    pieces = (layer_input, after_low, after_high, before_low, before_high)
    half = lax.dynamic_slice_in_dim(query_weight, core * HALF_FEATURES, HALF_FEATURES, 0)
    parcels = [
        jnp.concatenate([half, grads[k * PART : (k + 1) * PART]], 0) for k in (1, 2, 3)
    ]
    ready_grads, parcels[0], parcels[2] = lax.optimization_barrier(
        (grads, parcels[0], parcels[2])
    )
    started = started_merged(pieces, ready_grads, error)
    merged, mine, other = merged_and_left(
        core_word, far_low, far_high, grads, started, right_rows
    )

    parcels = lax.optimization_barrier((*parcels, before_high))[:3]
    before, after = shift(parcels[0], "tensor", 4, 1), shift(parcels[2], "tensor", 4, -1)

    total = (mine + shift(other, "c", 2, 1)).reshape(32, 7, 4, 128)
    blocks = lax.all_to_all(total, PLANE, 0, 0, tiled=True)
    blocks, before, after = lax.optimization_barrier((blocks, before, after))
    parcels = (before, shift(parcels[1], "tensor", 4, 2), after)
    copies = summed_copies(blocks, 32)
    mine = lax.all_to_all(copies, PLANE, 0, 0, tiled=True).reshape(TILES)
    other = shift(mine, "c", 2, 1)

    left, cross, gram = products(core_word, mine, other, merged)
    inverse = inverse_factor(gram)

    mine = lax.dynamic_slice_in_dim(cross, core * HALF, HALF, 0)
    other = lax.dynamic_slice_in_dim(cross, (1 - core) * HALF, HALF, 0)
    mine = (mine + shift(other, "c", 2, 1)) * (1 / REPLICAS)
    copies = jnp.broadcast_to(mine[None], (4, HALF, COLUMNS))
    mine = jnp.sum(lax.all_to_all(copies, "x", 0, 0, tiled=True), 0)

    mine, inverse, *parcels = lax.optimization_barrier((mine, inverse, *parcels))
    other_parcels = [shift(parcel, "c", 2, 1) for parcel in parcels]
    basis = orthonormal(inverse, left, 896)
    input_grad = input_gradient(core_word, grads[:PART], query_weight, parcels, other_parcels)

    copies = jnp.broadcast_to(mine[None], (8, HALF, COLUMNS))
    blocks = lax.all_to_all(copies, "z", 0, 0, tiled=True)
    blocks, basis, input_grad = lax.optimization_barrier((blocks, basis, input_grad))
    mine = jnp.sum(blocks, 0)
    other = shift(mine, "c", 2, 1)

    error_next, right = finish(core_word, mine, other, inverse, basis, merged, 896)
    return input_grad, right.T, error_next[None]


def solution(mesh):
    split = Mesh(mesh.devices.reshape(8, 4, 2, 4), ("z", "x", "c", "tensor"))
    dp = ("z", "x", "c")
    in_specs = (
        P((*dp, "tensor"), None),
        P(dp, "tensor"),
        P(None, "tensor"),
        P(dp, None, "tensor"),
        P("tensor", None),
    )
    out_specs = (P((*dp, "tensor"), None), P("tensor", None), P(dp, None, "tensor"))
    return jax.shard_map(
        shards, mesh=split, in_specs=in_specs, out_specs=out_specs, check_vma=False
    )
```

```python
import jax
import jax.numpy as jnp
from jax import lax
from jax.experimental import pallas as pl
from jax.experimental.pallas import tpu as pltpu
from jax.sharding import Mesh, PartitionSpec as P

F32, BF16 = jnp.float32, jnp.bfloat16
HIGHEST = lax.Precision.HIGHEST
FEATURES, COLUMNS, RANK, SEQ, PART = 3584, 256, 64, 768, 192
HALF = RANK // 2
REPLICAS = 64
STEP = 896
TILES = (8, 4, 7, 4, 128)
HALF_FEATURES = FEATURES // 2
PIVOTS = 8
PLANE = ("z", "x")
SMALL = pl.CostEstimate(flops=1000, bytes_accessed=1000, transcendentals=0)
VMEM = pltpu.CompilerParams(vmem_limit_bytes=40 * 2**20)
ALL_VMEM = pltpu.CompilerParams(vmem_limit_bytes=60 * 2**20)


def dot(a, b, dim_a, dim_b, precision=None):
    return lax.dot_general(
        a, b, (((dim_a,), (dim_b,)), ((), ())), precision=precision, preferred_element_type=F32
    )


def whole(array):
    return pl.BlockSpec(array.shape, lambda i: (0,) * array.ndim)


def shift(value, axis, size, by):
    return lax.ppermute(value, axis, [(at, (at + by) % size) for at in range(size)])


def split(value):
    high = value.astype(BF16)
    rest = value - high.astype(F32)
    middle = rest.astype(BF16)
    return high, middle, (rest - middle.astype(F32)).astype(BF16)


def stacked_dot(a, b, dim_b):
    rows = a.shape[0]
    stack = jnp.concatenate(split(a), 0)
    high, middle, low = split(b)
    first = dot(stack, high, 1, dim_b)
    second = dot(stack[: 2 * rows], middle, 1, dim_b)
    third = dot(stack[:rows], low, 1, dim_b)
    small = first[2 * rows :] + second[rows:] + third
    return first[:rows] + (first[rows : 2 * rows] + second[:rows] + small)


def started_merged(pieces, grads, error):
    def body(*refs):
        *piece_refs, grad_ref, error_ref, merged_ref = refs
        tokens = jnp.concatenate([ref[...] for ref in piece_refs], 0)
        near = jnp.concatenate([grad_ref[: 2 * PART], grad_ref[3 * PART :]], 0)
        merged_ref[...] = dot(near, tokens, 0, 0).T + error_ref[...].astype(F32)

    rows = pl.BlockSpec((STEP, COLUMNS), lambda i: (i, 0))
    return pl.pallas_call(
        body,
        grid=(FEATURES // STEP,),
        in_specs=[pl.BlockSpec((piece.shape[0], STEP), lambda i: (0, i)) for piece in pieces]
        + [whole(grads), rows],
        out_specs=rows,
        out_shape=jax.ShapeDtypeStruct((FEATURES, COLUMNS), F32),
        compiler_params=VMEM,
        cost_estimate=SMALL,
        name="started_merged",
    )(*pieces, grads, error)


def merged_and_left(core, far_low, far_high, grads, started, right):
    def body(core_ref, low_ref, high_ref, grad_ref, started_ref, right_ref, *refs):
        merged_ref, mine_ref, other_ref = refs
        tokens = jnp.concatenate([low_ref[...], high_ref[...]], 0)
        far = dot(grad_ref[2 * PART : 3 * PART], tokens, 0, 0)
        merged = far.T + started_ref[...]
        merged_ref[...] = merged
        left = stacked_dot(right_ref[...], merged, 1)
        low, high = left[:HALF], left[HALF:]
        is_first = core_ref[0] == 0
        mine, other = jnp.where(is_first, low, high), jnp.where(is_first, high, low)
        for row in range(8):
            for lane in range(7):
                tile = slice(row * 4, row * 4 + 4), slice(lane * 128, lane * 128 + 128)
                mine_ref[row, 0, lane] = mine[tile]
                other_ref[row, 0, lane] = other[tile]

    rows = pl.BlockSpec((STEP, COLUMNS), lambda i: (i, 0))
    columns = pl.BlockSpec((PART // 2, STEP), lambda i: (0, i))
    tiles = pl.BlockSpec((8, 1, 7, 4, 128), lambda i: (0, i, 0, 0, 0))
    return pl.pallas_call(
        body,
        grid=(FEATURES // STEP,),
        in_specs=[pl.BlockSpec(memory_space=pltpu.SMEM), columns, columns]
        + [whole(grads), rows, whole(right)],
        out_specs=[rows, tiles, tiles],
        out_shape=[
            jax.ShapeDtypeStruct((FEATURES, COLUMNS), F32),
            jax.ShapeDtypeStruct(TILES, F32),
            jax.ShapeDtypeStruct(TILES, F32),
        ],
        compiler_params=VMEM,
        cost_estimate=SMALL,
        name="merged_and_left",
    )(core, far_low, far_high, grads, started, right)


def ordered(core, mine, other):
    first = core == 0
    return jnp.concatenate([jnp.where(first, mine, other), jnp.where(first, other, mine)], 0)


def products(core, mine, other, merged):
    def body(core_ref, mine_ref, other_ref, merged_ref, left_ref, cross_ref, gram_ref):
        @pl.when(pl.program_id(0) == 0)
        def _():
            cross_ref[...] = jnp.zeros_like(cross_ref)
            gram_ref[...] = jnp.zeros_like(gram_ref)

        def rows(ref):
            return jnp.concatenate(
                [jnp.concatenate([ref[row, 0, lane] for lane in range(7)], 1) for row in range(8)],
                0,
            )

        left = ordered(core_ref[0], rows(mine_ref), rows(other_ref))
        left_ref[...] = left
        stack = jnp.concatenate(split(left), 0)
        squares = dot(stack, stack, 1, 1)

        def square(a, b):
            return squares[a * RANK : (a + 1) * RANK, b * RANK : (b + 1) * RANK]

        small = square(0, 2) + square(2, 0) + square(1, 1)
        gram_ref[...] += square(0, 0) + (square(0, 1) + square(1, 0) + small)
        cross_ref[...] += stacked_dot(left, merged_ref[...], 0)

    tiles = pl.BlockSpec((8, 1, 7, 4, 128), lambda i: (0, i, 0, 0, 0))
    return pl.pallas_call(
        body,
        grid=(FEATURES // STEP,),
        in_specs=[
            pl.BlockSpec(memory_space=pltpu.SMEM),
            tiles,
            tiles,
            pl.BlockSpec((STEP, COLUMNS), lambda i: (i, 0)),
        ],
        out_specs=[
            pl.BlockSpec((RANK, STEP), lambda i: (0, i)),
            pl.BlockSpec((RANK, COLUMNS), lambda i: (0, 0)),
            pl.BlockSpec((RANK, RANK), lambda i: (0, 0)),
        ],
        out_shape=[
            jax.ShapeDtypeStruct((RANK, FEATURES), F32),
            jax.ShapeDtypeStruct((RANK, COLUMNS), F32),
            jax.ShapeDtypeStruct((RANK, RANK), F32),
        ],
        compiler_params=VMEM,
        cost_estimate=SMALL,
        name="cross_and_gram",
    )(core, mine, other, merged)


def inverse_factor(gram):
    def body(gram_ref, inverse_ref):
        shape = (PIVOTS, 2 * RANK)
        rows = lax.broadcasted_iota(jnp.int32, (RANK, 2 * RANK), 0)
        lanes = lax.broadcasted_iota(jnp.int32, (RANK, 2 * RANK), 1)
        work = jnp.concatenate([gram_ref[...], jnp.zeros((RANK, RANK), F32)], 1)
        work = jnp.where(lanes == rows + RANK, 1.0, work)
        tiles = [work[at : at + PIVOTS] for at in range(0, RANK, PIVOTS)]
        local = lax.broadcasted_iota(jnp.int32, shape, 0)
        for at in range(len(tiles)):
            columns = [
                [
                    jnp.broadcast_to(tile[:, at * PIVOTS + k : at * PIVOTS + k + 1], shape)
                    for tile in tiles[at:]
                ]
                for k in range(PIVOTS)
            ]
            pivot_rows = [tiles[at][k : k + 1] for k in range(PIVOTS)]
            updates = [0.0] * len(tiles[at:])
            for k in range(PIVOTS):
                inverse = 1.0 / columns[k][0][k : k + 1]
                scaled = pivot_rows[k] * inverse
                for later in range(k + 1, PIVOTS):
                    pivot_rows[later] -= columns[k][0][later : later + 1] * scaled
                    factor = columns[later][0][k : k + 1] * inverse
                    columns[later] = [
                        column - done * factor
                        for column, done in zip(columns[later], columns[k])
                    ]
                updates = [update + done * scaled for update, done in zip(updates, columns[k])]
            for k in range(1, PIVOTS):
                tiles[at] = jnp.where(local == k, pivot_rows[k], tiles[at])
            for below in range(1, len(updates)):
                tiles[at + below] = tiles[at + below] - updates[below]
        work = jnp.concatenate(tiles, 0)
        pivots = jnp.sum(jnp.where(lanes == rows, work, 0.0), 1, keepdims=True)
        inverse_ref[...] = work[:, RANK:] * (1.0 / jnp.sqrt(pivots))

    return pl.pallas_call(
        body,
        out_shape=jax.ShapeDtypeStruct((RANK, RANK), F32),
        cost_estimate=SMALL,
        name="inverse_factor",
    )(gram)


def orthonormal(inverse, left, block):
    def body(inverse_ref, left_ref, basis_ref):
        basis = stacked_dot(inverse_ref[...], left_ref[...], 0).T
        high = basis.astype(BF16)
        low = (basis - high.astype(F32)).astype(BF16)
        basis_ref[...] = jnp.concatenate([high, low], 1)

    return pl.pallas_call(
        body,
        grid=(FEATURES // block,),
        in_specs=[whole(inverse), pl.BlockSpec((RANK, block), lambda i: (0, i))],
        out_specs=pl.BlockSpec((block, 2 * RANK), lambda i: (i, 0)),
        out_shape=jax.ShapeDtypeStruct((FEATURES, 2 * RANK), BF16),
        compiler_params=VMEM,
        cost_estimate=SMALL,
        name="orthonormal",
    )(inverse, left)


def finish(core, mine, other, inverse, basis, merged, block):
    def body(core_ref, mine_ref, other_ref, inverse_ref, basis_ref, merged_ref, *refs):
        error_ref, right_ref, parts_ref = refs

        @pl.when(pl.program_id(0) == 0)
        def _():
            cross = ordered(core_ref[0], mine_ref[...], other_ref[...])
            right = dot(inverse_ref[...], cross, 1, 0, HIGHEST)
            right_ref[...] = right
            high = right.astype(BF16)
            low = (right - high.astype(F32)).astype(BF16)
            parts_ref[...] = jnp.concatenate([high, high, low, low], 0)

        both = jnp.concatenate([basis_ref[...], basis_ref[...]], 1)
        approx = dot(both, parts_ref[...], 1, 0)
        error_ref[...] = (merged_ref[...] - approx).astype(BF16)

    rows = pl.BlockSpec((block, COLUMNS), lambda i: (i, 0))
    return pl.pallas_call(
        body,
        grid=(FEATURES // block,),
        in_specs=[
            pl.BlockSpec(memory_space=pltpu.SMEM),
            whole(mine),
            whole(other),
            whole(inverse),
            pl.BlockSpec((block, 2 * RANK), lambda i: (i, 0)),
            rows,
        ],
        out_specs=[rows, pl.BlockSpec((RANK, COLUMNS), lambda i: (0, 0))],
        out_shape=[
            jax.ShapeDtypeStruct((FEATURES, COLUMNS), BF16),
            jax.ShapeDtypeStruct((RANK, COLUMNS), F32),
        ],
        scratch_shapes=[pltpu.VMEM((4 * RANK, COLUMNS), BF16)],
        compiler_params=VMEM,
        cost_estimate=SMALL,
        name="finish",
    )(core, mine, other, inverse, basis, merged)


def input_gradient(core, grads, weight, mine, other):
    def body(core_ref, grad_ref, weight_ref, *refs):
        *parcel_refs, out_ref = refs

        def fill(halves):
            for first in range(0, HALF_FEATURES, 896):
                rows = slice(first, first + 896)
                total = dot(grad_ref[...], weight_ref[rows, :], 1, 1)
                for sent, weights in zip(parcel_refs, halves):
                    total = total + dot(sent[HALF_FEATURES:, :], weights[rows, :], 1, 1)
                out_ref[:, rows] = total.astype(BF16)

        @pl.when(pl.program_id(0) == 0)
        def _():
            fill(parcel_refs[:3])

        @pl.when(pl.program_id(0) == 1)
        def _():
            fill(parcel_refs[3:])

    def half(side, core_ref):
        return side + core_ref[0] * (1 - 2 * side)

    vmem = pl.BlockSpec(memory_space=pltpu.VMEM)
    return pl.pallas_call(
        body,
        grid_spec=pltpu.PrefetchScalarGridSpec(
            num_scalar_prefetch=1,
            grid=(2,),
            in_specs=[
                pl.BlockSpec((PART, COLUMNS), lambda side, core_ref: (0, 0)),
                pl.BlockSpec(
                    (HALF_FEATURES, COLUMNS), lambda side, core_ref: (half(side, core_ref), 0)
                ),
            ]
            + [vmem] * 6,
            out_specs=pl.BlockSpec(
                (PART, HALF_FEATURES), lambda side, core_ref: (0, half(side, core_ref))
            ),
        ),
        out_shape=jax.ShapeDtypeStruct((PART, FEATURES), BF16),
        compiler_params=VMEM,
        cost_estimate=SMALL,
        name="input_gradient",
    )(core, grads, weight, *mine, *other)


def summed_copies(blocks, count):
    def body(blocks_ref, copies_ref):
        mean = jnp.sum(blocks_ref[...], 0) * (1 / REPLICAS)
        copies_ref[...] = jnp.broadcast_to(mean[None], copies_ref.shape)

    return pl.pallas_call(
        body,
        out_shape=jax.ShapeDtypeStruct((count, *blocks.shape[1:]), F32),
        compiler_params=VMEM,
        cost_estimate=SMALL,
        name="summed_copies",
    )(blocks)


def row_halves(array):
    half = array.shape[0] // 2

    def body(array_ref, low_ref, high_ref, semaphores):
        copies = [
            pltpu.make_async_copy(array_ref.at[pl.ds(0, half)], low_ref, semaphores.at[0]),
            pltpu.make_async_copy(array_ref.at[pl.ds(half, half)], high_ref, semaphores.at[1]),
        ]
        for copy in copies:
            copy.start()
        for copy in copies:
            copy.wait()

    shape = jax.ShapeDtypeStruct((half, array.shape[1]), array.dtype)
    return pl.pallas_call(
        body,
        in_specs=[pl.BlockSpec(memory_space=pl.ANY)],
        out_specs=[pl.BlockSpec(memory_space=pl.ANY)] * 2,
        out_shape=[shape, shape],
        scratch_shapes=[pltpu.SemaphoreType.DMA((2,))],
        compiler_params=VMEM,
        cost_estimate=SMALL,
        name="row_halves",
    )(array)


def both_ways(value):
    return shift(value, "tensor", 4, 1), shift(value, "tensor", 4, -1)


def shards(layer_input, output_grad, query_weight, error_buffer, right_prev):
    core = lax.axis_index("c")
    place = lax.axis_index("tensor")
    error = error_buffer[0]
    core_word = core.astype(jnp.int32).reshape(1)

    grads = lax.dynamic_slice_in_dim(
        jnp.concatenate([output_grad, output_grad], 0), place * PART, SEQ, 0
    )
    right_rows = right_prev.T

    low, high = row_halves(layer_input)
    before_low, after_high = shift(low, "tensor", 4, 1), shift(high, "tensor", 4, -1)
    before_high, after_low = shift(high, "tensor", 4, 1), shift(low, "tensor", 4, -1)
    far_low, far_high = shift(before_low, "tensor", 4, 1), shift(after_high, "tensor", 4, -1)
    pieces = (layer_input, after_low, after_high, before_low, before_high)
    half = lax.dynamic_slice_in_dim(query_weight, core * HALF_FEATURES, HALF_FEATURES, 0)
    parcels = [
        jnp.concatenate([half, grads[k * PART : (k + 1) * PART]], 0) for k in (1, 2, 3)
    ]
    ready_grads, parcels[0], parcels[2] = lax.optimization_barrier(
        (grads, parcels[0], parcels[2])
    )
    started = started_merged(pieces, ready_grads, error)
    merged, mine, other = merged_and_left(
        core_word, far_low, far_high, grads, started, right_rows
    )

    parcels = lax.optimization_barrier((*parcels, before_high))[:3]
    before, after = shift(parcels[0], "tensor", 4, 1), shift(parcels[2], "tensor", 4, -1)

    total = (mine + shift(other, "c", 2, 1)).reshape(32, 7, 4, 128)
    blocks = lax.all_to_all(total, PLANE, 0, 0, tiled=True)
    blocks, before, after = lax.optimization_barrier((blocks, before, after))
    parcels = (before, shift(parcels[1], "tensor", 4, 2), after)
    copies = summed_copies(blocks, 32)
    mine = lax.all_to_all(copies, PLANE, 0, 0, tiled=True).reshape(TILES)
    other = shift(mine, "c", 2, 1)

    left, cross, gram = products(core_word, mine, other, merged)
    inverse = inverse_factor(gram)

    mine = lax.dynamic_slice_in_dim(cross, core * HALF, HALF, 0)
    other = lax.dynamic_slice_in_dim(cross, (1 - core) * HALF, HALF, 0)
    mine = (mine + shift(other, "c", 2, 1)) * (1 / REPLICAS)
    copies = jnp.broadcast_to(mine[None], (4, HALF, COLUMNS))
    mine = jnp.sum(lax.all_to_all(copies, "x", 0, 0, tiled=True), 0)

    mine, inverse, *parcels = lax.optimization_barrier((mine, inverse, *parcels))
    other_parcels = [shift(parcel, "c", 2, 1) for parcel in parcels]
    basis = orthonormal(inverse, left, 896)
    input_grad = input_gradient(core_word, grads[:PART], query_weight, parcels, other_parcels)

    copies = jnp.broadcast_to(mine[None], (8, HALF, COLUMNS))
    blocks = lax.all_to_all(copies, "z", 0, 0, tiled=True)
    blocks, basis, input_grad = lax.optimization_barrier((blocks, basis, input_grad))
    mine = jnp.sum(blocks, 0)
    other = shift(mine, "c", 2, 1)

    error_next, right = finish(core_word, mine, other, inverse, basis, merged, 896)
    return input_grad, right.T, error_next[None]


def solution(mesh):
    split = Mesh(mesh.devices.reshape(8, 4, 2, 4), ("z", "x", "c", "tensor"))
    dp = ("z", "x", "c")
    in_specs = (
        P((*dp, "tensor"), None),
        P(dp, "tensor"),
        P(None, "tensor"),
        P(dp, None, "tensor"),
        P("tensor", None),
    )
    out_specs = (P((*dp, "tensor"), None), P("tensor", None), P(dp, None, "tensor"))
    return jax.shard_map(
        shards, mesh=split, in_specs=in_specs, out_specs=out_specs, check_vma=False
    )
```
